512 devices in a mesh: island: 16 (over z, x_lo), shard: 32 (over y, x_hi, core).
Axes of the slice: x: 4 (x_hi: 2, x_lo: 2; x = x_hi * 2 + x_lo), y: 8, z: 8, core: 2. Of those that a mesh axis runs over, the one named last changes fastest.
Arguments:
- island_params: float32 [16, 2, 256, 4096], P('island', None, 'shard'), may hold values from -6 to 6
- outer_params: float32 [16, 1, 256, 4096], P('island', None, 'shard'), may hold values from -6 to 6
- momentum: float32 [16, 1, 256, 4096], P('island', None, 'shard'), may hold values from -3 to 3
- path_modules: int32 [16, 2], replicated, may hold values from 0 to 15, as said below
- owner_modules: int32 [16, 1], replicated, may hold values from 0 to 15, as said below
Outputs:
- new_params: float32 [16, 2, 256, 4096], P('island', None, 'shard')
- new_outer: float32 [16, 1, 256, 4096], P('island', None, 'shard')
- new_momentum: float32 [16, 1, 256, 4096], P('island', None, 'shard')
The draws below stay inside these ranges and needn't reach their ends.
Inputs may be any that keep to these rules, and one draw needn't show every extreme that they name: `path_modules`: column 0 names the level-one module (below 8) of island i's path and column 1 its level-two module (from 8 on); in each level some module is named by no island. `owner_modules`: every module stands in exactly one slot of one island.
All inputs are finite; a program needn't handle non-finite values.
Results may differ from the reference program's by a relative error of at most 0.00002.
Values sent between devices are 32-bit elements; how exact they have to be, the bound alone decides.
A program may use at most 64 MiB of HBM per device.

```python
import jax
import jax.numpy as jnp

D = 4096
NMOD = 16
ROWS = 256
OWN = 1
N_ISLAND = 16


def paired_island(key):
    return jax.random.randint(jax.random.fold_in(key, 5), (), 0, N_ISLAND).astype(jnp.int32)


def level_choice(key, forced_module, level_size, forced_island):
    unused_key, shuffle_key, left_key, right_key = jax.random.split(key, 4)
    unused = (forced_module + 1 + jax.random.randint(unused_key, (), 0, level_size - 1)) % level_size
    shuffled = jax.random.permutation(shuffle_key, level_size - 1).astype(jnp.int32)
    draw_left = jax.random.randint(left_key, (N_ISLAND,), 0, level_size - 1)
    draw_right = jax.random.randint(right_key, (N_ISLAND,), 0, level_size - 1)
    skew_rank = jnp.minimum(draw_left, draw_right)
    chosen = (unused + 1 + shuffled[skew_rank]) % level_size
    island_ids = jnp.arange(N_ISLAND, dtype=jnp.int32)
    return jnp.where(island_ids == forced_island, forced_module, chosen).astype(jnp.int32)


def draw_path_modules(key, part):
    first_island = paired_island(key)
    key = jax.random.fold_in(key, 11)
    level_one_key, level_two_key, second_key = jax.random.split(key, 3)
    second_island = jax.random.randint(second_key, (), 0, N_ISLAND).astype(jnp.int32)
    level_size = NMOD // 2
    level_one = level_choice(level_one_key, 0, level_size, first_island)
    level_two = level_size + level_choice(level_two_key, level_size - 1, level_size, second_island)
    return jnp.stack([level_one, level_two], axis=1).astype(jnp.int32)


def draw_owner_modules(key, part):
    first_island = paired_island(key)
    key = jax.random.fold_in(key, 23)
    shuffled = jax.random.permutation(key, NMOD).astype(jnp.int32)
    owner_island = (first_island + N_ISLAND // 2) % N_ISLAND
    target = owner_island * (NMOD // N_ISLAND)
    slot_ids = jnp.arange(NMOD, dtype=jnp.int32)
    held = jnp.sum(jnp.where(slot_ids == target, shuffled, 0))
    placed = jnp.where(slot_ids == target, 0, jnp.where(shuffled == 0, held, shuffled))
    return placed.astype(jnp.int32).reshape(N_ISLAND, NMOD // N_ISLAND)


def level_of(rng, shape, pieces, least, largest):
    gain, own = 1.0, jax.random.fold_in(rng, 6)
    for dim, shards_of in pieces:
        heights = jnp.exp(jax.random.uniform(jax.random.fold_in(own, dim), (shards_of,), jnp.float32, least / len(pieces), largest / len(pieces)))
        gain = gain * jnp.repeat(heights, shape[dim] // shards_of).reshape([-1 if axis == dim else 1 for axis in range(len(shape))])
    return gain


def noise(own_key, shape, scale, bound, shards=(), kind=jnp.bfloat16):
    values = jax.random.normal(own_key, shape, jnp.float32) * scale
    if len(shards) > 0:
        values = level_of(own_key, shape, shards, -0.22, 0.18) * values
    return jnp.clip(values, min=-bound, max=bound).astype(kind)


def setup_inputs(seed: int = 0) -> dict:
    splits = jax.random.split(jax.random.key(seed), 6)
    return {
        "island_params": noise(splits[0], (N_ISLAND, 2, ROWS, D), 1.0, 6.0, ((0, 16), (2, 32)), jnp.float32),
        "outer_params": noise(splits[1], (N_ISLAND, OWN, ROWS, D), 1.0, 6.0, ((0, 16), (2, 32)), jnp.float32),
        "momentum": noise(splits[2], (N_ISLAND, OWN, ROWS, D), 0.5, 3.0, ((0, 16), (2, 32)), jnp.float32),
        "path_modules": draw_path_modules(jax.random.fold_in(splits[5], 71), 0),
        "owner_modules": draw_owner_modules(jax.random.fold_in(splits[5], 71), 0),
    }


momentum_rate = 0.9
outer_rate = 0.7


def reference(island_params, outer_params, momentum, path_modules, owner_modules):
    module_ids = jnp.arange(NMOD, dtype=jnp.int32)
    usage_hits = (path_modules[:, :, None] == module_ids[None, None, :]).astype(jnp.float32)
    sharers = jnp.sum(usage_hits, axis=(0, 1))
    full_shape = (NMOD, ROWS, D)
    summed = jnp.zeros(full_shape, jnp.float32).at[path_modules.reshape(-1)].add(island_params.reshape(full_shape[:0] + (-1, ROWS, D)))
    flat_owned = owner_modules.reshape(-1)
    outer_full = jnp.zeros(full_shape, jnp.float32).at[flat_owned].set(outer_params.reshape(full_shape))
    slot_moment = jnp.zeros(full_shape, jnp.float32).at[flat_owned].set(momentum.reshape(full_shape))
    weight = sharers[:, None, None]
    pseudo_grad = (weight * outer_full - summed) / jnp.maximum(weight, 1.0)
    moment = momentum_rate * slot_moment + pseudo_grad
    updated = outer_full - outer_rate * (pseudo_grad + momentum_rate * moment)
    new_params = updated[path_modules]
    new_outer = updated[flat_owned].reshape(outer_params.shape)
    new_momentum = moment[flat_owned].reshape(momentum.shape)
    return new_params, new_outer, new_momentum
```

```python
import functools

import jax
import jax.numpy as jnp
from jax import lax
from jax.experimental import pallas as pl
from jax.experimental.pallas import tpu as pltpu
from jax.sharding import PartitionSpec as P

momentum_rate = 0.9
outer_rate = 0.7
MESH = pl.DeviceIdType.MESH


def kernel(n, p_hbm, outer_hbm, mom_hbm, path, owner, par_out, outer_out, mom_out,
           p_v, outer_v, mom_v, base_v, arrived, table, stage, home, moment_v, weights, slot_of,
           load_sem, store_sem, send_p, recv_p, send_b, recv_b, send_u, recv_u):
    me = lax.axis_index("island")
    depth = p_v.shape[1]
    cols = p_v.shape[2] // n
    pairs = [(dz, dx) for dz in (4, 3, 5, 2, 6, 1, 7, 0) for dx in (1, 0)]
    offsets = [(dz % (n // 2), dx) for dz, dx in pairs if (dz % (n // 2), dx) != (0, 0)]
    z, x = me // 2, me % 2

    def ahead(k):
        dz, dx = offsets[k]
        return lax.rem(z + dz, n // 2) * 2 + lax.rem(x + dx, 2)

    def behind(k):
        dz, dx = offsets[k]
        return lax.rem(z + n // 2 - dz, n // 2) * 2 + lax.rem(x + dx, 2)

    peers = len(offsets)

    def span(j):
        return pl.ds(pl.multiple_of(j * cols, cols), cols)

    loads = [pltpu.make_async_copy(a, b, load_sem.at[i]) for i, (a, b) in enumerate(
        ((p_hbm.at[0], p_v), (outer_hbm.at[0, 0], outer_v), (mom_hbm.at[0, 0], mom_v)))]
    for c in loads:
        c.start()
    barrier = pltpu.get_barrier_semaphore()
    for k in range(peers):
        pl.semaphore_signal(barrier, inc=1, device_id={"island": ahead(k)}, device_id_type=MESH)
    pl.semaphore_wait(barrier, peers)
    loads[0].wait()

    def remote(src, dst, ssem, rsem, k):
        return pltpu.make_async_remote_copy(src_ref=src, dst_ref=dst, send_sem=ssem, recv_sem=rsem,
                                            device_id={"island": ahead(k)}, device_id_type=MESH)

    sends = []
    for k in range(peers):
        c = remote(p_v.at[:, :, span(ahead(k))], arrived.at[k, 0:2], send_p.at[k], recv_p.at[k], k)
        c.start()
        sends.append(c)
    loads[1].wait()
    loads[2].wait()
    mine = owner[me, 0]
    used = jnp.int32(0)
    for j in range(n):
        for l in range(2):
            used += (path[j, l] == mine).astype(jnp.int32)
    hit = jnp.minimum(used, 1).astype(jnp.float32)
    keep = 1.0 - outer_rate * (1.0 + momentum_rate) * hit
    base_v[...] = keep * outer_v[...] - (outer_rate * momentum_rate * momentum_rate) * mom_v[...]
    for k in range(peers):
        c = remote(base_v.at[:, span(ahead(k))], arrived.at[k, 2], send_b.at[k], recv_b.at[k], k)
        c.start()
        sends.append(c)
    arrived[peers, 0:2] = p_v[:, :, span(me)]
    arrived[peers, 2] = base_v[:, span(me)]

    sources = [behind(k) for k in range(peers)] + [me]
    for m in range(n):
        level = m // (n // 2)
        count = jnp.int32(0)
        holder = jnp.int32(0)
        for k in range(n):
            count += (path[sources[k], level] == m).astype(jnp.int32)
            holder = jnp.where(owner[sources[k], 0] == m, jnp.int32(k), holder)
        slot_of[m] = holder
        rate = outer_rate * (1.0 + momentum_rate) / jnp.maximum(
            jnp.full((1, 128), count.astype(jnp.float32)), 1.0)
        for k in range(n):
            f = (path[sources[k], level] == m).astype(jnp.float32)
            weights[pl.ds(m * n + k, 1), :] = rate * f

    for k in range(peers):
        remote(p_v.at[:, :, span(me)], arrived.at[k, 0:2], send_p.at[k], recv_p.at[k], k).wait_recv()
    for k in range(peers):
        remote(base_v.at[:, span(me)], arrived.at[k, 2], send_b.at[k], recv_b.at[k], k).wait_recv()

    half = n // 2
    for level in range(2):
        acc = [arrived[slot_of[level * half + m], 2] for m in range(half)]
        for k in range(n):
            v = arrived[k, level]
            for m in range(half):
                w = weights[pl.ds((level * half + m) * n + k, 1), :]
                w = jnp.concatenate([w] * (cols // 128), axis=1)
                acc[m] = acc[m] + w * v
        for m in range(half):
            table[level * half + m] = acc[m]

    for k in range(peers):
        to = ahead(k)
        stage[k, 0] = table[path[to, 0]]
        stage[k, 1] = table[path[to, 1]]
        stage[k, 2] = table[owner[to, 0]]
        c = remote(stage.at[k], home.at[:, :, span(me)], send_u.at[k], recv_u.at[k], k)
        c.start()
        sends.append(c)
    home[0, :, span(me)] = table[path[me, 0]]
    home[1, :, span(me)] = table[path[me, 1]]
    home[2, :, span(me)] = table[owner[me, 0]]
    for k in range(peers):
        remote(stage.at[k], home.at[:, :, span(behind(k))], send_u.at[k], recv_u.at[k], k).wait_recv()
    stores = [pltpu.make_async_copy(home.at[0:2], par_out.at[0], store_sem.at[0]),
              pltpu.make_async_copy(home.at[2], outer_out.at[0, 0], store_sem.at[1]),
              pltpu.make_async_copy(moment_v, mom_out.at[0, 0], store_sem.at[2])]
    stores[0].start()
    stores[1].start()
    moment_v[...] = ((outer_v[...] - home[2]) * (1.0 / outer_rate) + momentum_rate * mom_v[...]) * (
        1.0 / (1.0 + momentum_rate))
    stores[2].start()
    for c in sends:
        c.wait_send()
    for c in stores:
        c.wait()


def body(island_params, outer_params, momentum, path_modules, owner_modules):
    n = path_modules.shape[0]
    depth, width = island_params.shape[2:]
    cols = width // n
    f32 = jnp.float32
    any_ = pl.BlockSpec(memory_space=pl.ANY)
    smem = pl.BlockSpec(memory_space=pltpu.SMEM)
    return pl.pallas_call(
        functools.partial(kernel, n),
        out_shape=(jax.ShapeDtypeStruct(island_params.shape, f32),
                   jax.ShapeDtypeStruct(outer_params.shape, f32),
                   jax.ShapeDtypeStruct(momentum.shape, f32)),
        in_specs=[any_, any_, any_, smem, smem],
        out_specs=(any_, any_, any_),
        scratch_shapes=[
            pltpu.VMEM((2, depth, width), f32),
            pltpu.VMEM((depth, width), f32),
            pltpu.VMEM((depth, width), f32),
            pltpu.VMEM((depth, width), f32),
            pltpu.VMEM((n, 3, depth, cols), f32),
            pltpu.VMEM((n, depth, cols), f32),
            pltpu.VMEM((n, 3, depth, cols), f32),
            pltpu.VMEM((3, depth, width), f32),
            pltpu.VMEM((depth, width), f32),
            pltpu.VMEM((n * n, 128), f32),
            pltpu.SMEM((n,), jnp.int32),
            pltpu.SemaphoreType.DMA((3,)),
            pltpu.SemaphoreType.DMA((3,)),
        ] + [pltpu.SemaphoreType.DMA((n,))] * 6,
        compiler_params=pltpu.CompilerParams(collective_id=1, has_side_effects=True,
                                             vmem_limit_bytes=16 * 1024 * 1024),
        name="outer_step",
    )(island_params, outer_params, momentum, path_modules, owner_modules)


def solution(mesh):
    split = P("island", None, "shard", None)
    return jax.shard_map(
        body,
        mesh=mesh,
        in_specs=(split, split, split, P(), P()),
        out_specs=(split, split, split),
        check_vma=False,
    )
```

```python
import functools

import jax
import jax.numpy as jnp
from jax import lax
from jax.experimental import pallas as pl
from jax.experimental.pallas import tpu as pltpu
from jax.sharding import PartitionSpec as P

momentum_rate = 0.9
outer_rate = 0.7
both_rates = outer_rate * (1.0 + momentum_rate)
MESH = pl.DeviceIdType.MESH
ROOM = 60 * 1024 * 1024
chunks = 2


def relay(n, p_hbm, outer_hbm, mom_hbm, path_hbm, owner_hbm, home,
          path, owner, outer_v, mom_v, base_v, table, stage, weights, slot_of,
          load_sem, self_sem, send_p, recv_p, send_b, recv_b, send_u, recv_u, *arrived):
    me = lax.axis_index("island")
    ring = n // 2
    width = outer_v.shape[1]
    cols = width // n // chunks
    far_first = sorted(range(ring), key=lambda d: -min(d, ring - d))
    offsets = [(dz, dx) for dz in far_first for dx in (1, 0) if (dz, dx) != (0, 0)]
    peers = len(offsets)
    z, x = me // 2, me % 2

    def ahead(k):
        dz, dx = offsets[k]
        return lax.rem(z + dz, ring) * 2 + lax.rem(x + dx, 2)

    def behind(k):
        dz, dx = offsets[k]
        return lax.rem(z + ring - dz, ring) * 2 + lax.rem(x + dx, 2)

    def span(j, c):
        return pl.ds(pl.multiple_of(j * (cols * chunks) + c * cols, cols), cols)

    def remote(src, dst, ssem, rsem, k):
        return pltpu.make_async_remote_copy(
            src_ref=src, dst_ref=dst, send_sem=ssem, recv_sem=rsem,
            device_id={"island": ahead(k)}, device_id_type=MESH)

    def drain(ref, sem):
        pltpu.make_async_copy(ref, ref, sem).wait()

    small = [pltpu.make_async_copy(path_hbm, path, load_sem.at[0]),
             pltpu.make_async_copy(owner_hbm, owner, load_sem.at[1]),
             pltpu.make_async_copy(outer_hbm.at[0, 0], outer_v, load_sem.at[2]),
             pltpu.make_async_copy(mom_hbm.at[0, 0], mom_v, load_sem.at[3])]
    own = [pltpu.make_async_copy(p_hbm.at[0, :, :, span(me, c)], arrived[c].at[peers, 0:2], self_sem.at[c])
           for c in range(chunks)]
    for copy in small + own:
        copy.start()
    barrier = pltpu.get_barrier_semaphore()
    for k in range(peers):
        pl.semaphore_signal(barrier, inc=1, device_id={"island": ahead(k)}, device_id_type=MESH)
    pl.semaphore_wait(barrier, peers)

    def send_params(c):
        for k in range(peers):
            remote(p_hbm.at[0, :, :, span(ahead(k), c)], arrived[c].at[k, 0:2],
                   send_p.at[c], recv_p.at[c], k).start()

    def send_base(c):
        for k in range(peers):
            remote(base_v.at[:, span(ahead(k), c)], arrived[c].at[k, 2],
                   send_b.at[c], recv_b.at[c], k).start()

    send_params(0)
    for copy in small:
        copy.wait()
    mine = owner[0, me]
    used = jnp.int32(0)
    for j in range(n):
        for level in range(2):
            used += (path[level, j] == mine).astype(jnp.int32)
    hit = jnp.minimum(used, 1).astype(jnp.float32)
    base_v[...] = (1.0 - both_rates * hit) * outer_v[...] - (
        outer_rate * momentum_rate * momentum_rate) * mom_v[...]
    send_base(0)
    for c in range(1, chunks):
        send_params(c)
        send_base(c)
    for c in range(chunks):
        arrived[c][peers, 2] = base_v[:, span(me, c)]

    sources = [behind(k) for k in range(peers)] + [me]
    for m in range(n):
        level = m // ring
        count = jnp.int32(0)
        holder = jnp.int32(0)
        for k in range(n):
            count += (path[level, sources[k]] == m).astype(jnp.int32)
            holder = jnp.where(owner[0, sources[k]] == m, jnp.int32(k), holder)
        slot_of[m] = holder
        rate = both_rates / jnp.maximum(jnp.full((1, 128), count.astype(jnp.float32)), 1.0)
        for k in range(n):
            weights[pl.ds(m * n + k, 1), :] = rate * (path[level, sources[k]] == m).astype(jnp.float32)

    for c in range(chunks):
        own[c].wait()
        drain(arrived[c].at[0:peers, 0:2], recv_p.at[c])
        drain(arrived[c].at[0:peers, 2], recv_b.at[c])
        for level in range(2):
            acc = [arrived[c][slot_of[level * ring + m], 2] for m in range(ring)]
            for k in range(n):
                v = arrived[c][k, level]
                for m in range(ring):
                    w = weights[pl.ds((level * ring + m) * n + k, 1), :]
                    if cols > 128:
                        w = jnp.concatenate([w] * (cols // 128), axis=1)
                    acc[m] = acc[m] + w * v
            for m in range(ring):
                table[c, level * ring + m] = acc[m]
        for k in range(n):
            to = ahead(k) if k < peers else me
            stage[c, k, 0] = table[c, path[0, to]]
            stage[c, k, 1] = table[c, path[1, to]]
            stage[c, k, 2] = table[c, owner[0, to]]
            if k < peers:
                remote(stage.at[c, k], home.at[:, :, span(me, c)], send_u.at[c], recv_u.at[c], k).start()
        pltpu.make_async_copy(stage.at[c, peers], home.at[:, :, span(me, c)], self_sem.at[c]).start()
    for c in range(chunks):
        pltpu.make_async_copy(stage.at[c, peers], home.at[:, :, span(me, c)], self_sem.at[c]).wait()
        drain(stage.at[c, 0:peers], recv_u.at[c])
    for c in range(chunks):
        drain(arrived[c].at[0:peers, 0:2], send_p.at[c])
        drain(arrived[c].at[0:peers, 2], send_b.at[c])
        drain(stage.at[c, 0:peers], send_u.at[c])


def finish(home, outer_hbm, mom_hbm, par_out, outer_out, mom_out, home_v, outer_v, mom_v, new_v, load_sem, store_sem):
    loads = [pltpu.make_async_copy(home.at[2], home_v.at[2], load_sem.at[0]),
             pltpu.make_async_copy(outer_hbm.at[0, 0], outer_v, load_sem.at[1]),
             pltpu.make_async_copy(mom_hbm.at[0, 0], mom_v, load_sem.at[2]),
             pltpu.make_async_copy(home.at[0], home_v.at[0], load_sem.at[3]),
             pltpu.make_async_copy(home.at[1], home_v.at[1], load_sem.at[4])]
    stores = [pltpu.make_async_copy(home_v.at[2], outer_out.at[0, 0], store_sem.at[0]),
              pltpu.make_async_copy(home_v.at[0], par_out.at[0, 0], store_sem.at[1]),
              pltpu.make_async_copy(home_v.at[1], par_out.at[0, 1], store_sem.at[2]),
              pltpu.make_async_copy(new_v, mom_out.at[0, 0], store_sem.at[3])]
    for copy in loads:
        copy.start()
    loads[0].wait()
    stores[0].start()
    loads[1].wait()
    loads[2].wait()
    new_v[...] = ((outer_v[...] - home_v[2]) * (1.0 / outer_rate) + momentum_rate * mom_v[...]) * (
        1.0 / (1.0 + momentum_rate))
    stores[3].start()
    loads[3].wait()
    stores[1].start()
    loads[4].wait()
    stores[2].start()
    for copy in stores:
        copy.wait()


def body(island_params, outer_params, momentum, path_modules, owner_modules):
    n = path_modules.shape[0]
    depth, width = island_params.shape[2:]
    cols = width // n // chunks
    f32 = jnp.float32
    hbm = pl.BlockSpec(memory_space=pltpu.HBM)
    dma = pltpu.SemaphoreType.DMA
    home = pl.pallas_call(
        functools.partial(relay, n),
        out_shape=jax.ShapeDtypeStruct((3, depth, width), f32),
        in_specs=[hbm] * 5,
        out_specs=hbm,
        scratch_shapes=[
            pltpu.SMEM((2, n), jnp.int32),
            pltpu.SMEM((1, n), jnp.int32),
            pltpu.VMEM((depth, width), f32),
            pltpu.VMEM((depth, width), f32),
            pltpu.VMEM((depth, width), f32),
            pltpu.VMEM((chunks, n, depth, cols), f32),
            pltpu.VMEM((chunks, n, 3, depth, cols), f32),
            pltpu.VMEM((n * n, 128), f32),
            pltpu.SMEM((n,), jnp.int32),
            dma((4,)),
        ] + [dma((chunks,))] * 7 + [pltpu.VMEM((n, 3, depth, cols), f32)] * chunks,
        compiler_params=pltpu.CompilerParams(collective_id=1, has_side_effects=True, vmem_limit_bytes=ROOM),
        name="outer_step",
    )(island_params, outer_params, momentum, path_modules.T, owner_modules.T)
    return pl.pallas_call(
        finish,
        out_shape=tuple(jax.ShapeDtypeStruct(a.shape, f32) for a in (island_params, outer_params, momentum)),
        in_specs=[hbm] * 3,
        out_specs=(hbm,) * 3,
        scratch_shapes=[
            pltpu.VMEM((3, depth, width), f32),
            pltpu.VMEM((depth, width), f32),
            pltpu.VMEM((depth, width), f32),
            pltpu.VMEM((depth, width), f32),
            dma((5,)),
            dma((4,)),
        ],
        compiler_params=pltpu.CompilerParams(vmem_limit_bytes=ROOM),
        name="finish",
    )(home, outer_params, momentum)


def solution(mesh):
    split = P("island", None, "shard", None)
    return jax.shard_map(
        body,
        mesh=mesh,
        in_specs=(split, split, split, P(), P()),
        out_specs=(split, split, split),
        check_vma=False,
    )
```

```python
import functools

import jax
import jax.numpy as jnp
from jax import lax
from jax.experimental import pallas as pl
from jax.experimental.pallas import tpu as pltpu
from jax.sharding import PartitionSpec as P

momentum_rate = 0.9
outer_rate = 0.7
both_rates = outer_rate * (1.0 + momentum_rate)
MESH = pl.DeviceIdType.MESH
ROOM = 16 * 1024 * 1024
chunks = 2


def relay(n, p_hbm, outer_hbm, mom_hbm, path_hbm, owner_hbm, home,
          path, owner, outer_v, mom_v, base_v, table, stage, weights, slot_of,
          load_sem, self_sem, send_p, recv_p, send_b, recv_b, send_u, recv_u, *arrived):
    me = lax.axis_index("island")
    ring = n // 2
    width = outer_v.shape[1]
    cols = width // n // chunks
    far_first = sorted(range(ring), key=lambda d: -min(d, ring - d))
    offsets = [(dz, dx) for dz in far_first for dx in (1, 0) if (dz, dx) != (0, 0)]
    peers = len(offsets)
    z, x = me // 2, me % 2

    def ahead(k):
        dz, dx = offsets[k]
        return lax.rem(z + dz, ring) * 2 + lax.rem(x + dx, 2)

    def behind(k):
        dz, dx = offsets[k]
        return lax.rem(z + ring - dz, ring) * 2 + lax.rem(x + dx, 2)

    def span(j, c):
        return pl.ds(pl.multiple_of(j * (cols * chunks) + c * cols, cols), cols)

    def remote(src, dst, ssem, rsem, k):
        return pltpu.make_async_remote_copy(
            src_ref=src, dst_ref=dst, send_sem=ssem, recv_sem=rsem,
            device_id={"island": ahead(k)}, device_id_type=MESH)

    def drain(ref, sem):
        pltpu.make_async_copy(ref, ref, sem).wait()

    small = [pltpu.make_async_copy(path_hbm, path, load_sem.at[0]),
             pltpu.make_async_copy(owner_hbm, owner, load_sem.at[1]),
             pltpu.make_async_copy(outer_hbm.at[0, 0], outer_v, load_sem.at[2]),
             pltpu.make_async_copy(mom_hbm.at[0, 0], mom_v, load_sem.at[3])]
    own = [pltpu.make_async_copy(p_hbm.at[0, :, :, span(me, c)], arrived[c].at[peers, 0:2], self_sem.at[c])
           for c in range(chunks)]
    for copy in small + own:
        copy.start()
    barrier = pltpu.get_barrier_semaphore()
    for k in range(peers):
        pl.semaphore_signal(barrier, inc=1, device_id={"island": ahead(k)}, device_id_type=MESH)
    pl.semaphore_wait(barrier, peers)

    def send_params(c):
        for k in range(peers):
            remote(p_hbm.at[0, :, :, span(ahead(k), c)], arrived[c].at[k, 0:2],
                   send_p.at[c], recv_p.at[c], k).start()

    def send_base(c):
        for k in range(peers):
            remote(base_v.at[:, span(ahead(k), c)], arrived[c].at[k, 2],
                   send_b.at[c], recv_b.at[c], k).start()

    send_params(0)
    for copy in small:
        copy.wait()
    mine = owner[0, me]
    used = jnp.int32(0)
    for j in range(n):
        for level in range(2):
            used += (path[level, j] == mine).astype(jnp.int32)
    hit = jnp.minimum(used, 1).astype(jnp.float32)
    base_v[...] = (1.0 - both_rates * hit) * outer_v[...] - (
        outer_rate * momentum_rate * momentum_rate) * mom_v[...]
    send_base(0)
    for c in range(1, chunks):
        send_params(c)
        send_base(c)
    for c in range(chunks):
        arrived[c][peers, 2] = base_v[:, span(me, c)]

    sources = [behind(k) for k in range(peers)] + [me]
    for m in range(n):
        level = m // ring
        count = jnp.int32(0)
        holder = jnp.int32(0)
        for k in range(n):
            count += (path[level, sources[k]] == m).astype(jnp.int32)
            holder = jnp.where(owner[0, sources[k]] == m, jnp.int32(k), holder)
        slot_of[m] = holder
        rate = both_rates / jnp.maximum(jnp.full((1, 128), count.astype(jnp.float32)), 1.0)
        for k in range(n):
            weights[pl.ds(m * n + k, 1), :] = rate * (path[level, sources[k]] == m).astype(jnp.float32)

    for c in range(chunks):
        own[c].wait()
        drain(arrived[c].at[0:peers, 0:2], recv_p.at[c])
        drain(arrived[c].at[0:peers, 2], recv_b.at[c])
        for level in range(2):
            acc = [arrived[c][slot_of[level * ring + m], 2] for m in range(ring)]
            for k in range(n):
                v = arrived[c][k, level]
                for m in range(ring):
                    w = weights[pl.ds((level * ring + m) * n + k, 1), :]
                    if cols > 128:
                        w = jnp.concatenate([w] * (cols // 128), axis=1)
                    acc[m] = acc[m] + w * v
            for m in range(ring):
                table[c, level * ring + m] = acc[m]
        for k in range(n):
            to = ahead(k) if k < peers else me
            stage[c, k, 0] = table[c, path[0, to]]
            stage[c, k, 1] = table[c, path[1, to]]
            stage[c, k, 2] = table[c, owner[0, to]]
            if k < peers:
                remote(stage.at[c, k], home.at[0:3, :, span(me, c)], send_u.at[c], recv_u.at[c], k).start()
        pltpu.make_async_copy(stage.at[c, peers], home.at[0:3, :, span(me, c)], self_sem.at[c]).start()
    for c in range(chunks):
        pltpu.make_async_copy(stage.at[c, peers], home.at[0:3, :, span(me, c)], self_sem.at[c]).wait()
        drain(stage.at[c, 0:peers], recv_u.at[c])
    home[3] = ((outer_v[...] - home[2]) * (1.0 / outer_rate) + momentum_rate * mom_v[...]) * (
        1.0 / (1.0 + momentum_rate))
    for c in range(chunks):
        drain(arrived[c].at[0:peers, 0:2], send_p.at[c])
        drain(arrived[c].at[0:peers, 2], send_b.at[c])
        drain(stage.at[c, 0:peers], send_u.at[c])


def finish(home, par_out, outer_out, mom_out, sem):
    stores = [pltpu.make_async_copy(home.at[0:2], par_out.at[0], sem.at[0]),
              pltpu.make_async_copy(home.at[2], outer_out.at[0, 0], sem.at[1]),
              pltpu.make_async_copy(home.at[3], mom_out.at[0, 0], sem.at[2])]
    for copy in stores:
        copy.start()
    for copy in stores:
        copy.wait()


def body(island_params, outer_params, momentum, path_modules, owner_modules):
    n = path_modules.shape[0]
    depth, width = island_params.shape[2:]
    cols = width // n // chunks
    f32 = jnp.float32
    hbm = pl.BlockSpec(memory_space=pltpu.HBM)
    dma = pltpu.SemaphoreType.DMA
    ins = [pltpu.with_memory_space_constraint(a, pltpu.HBM) for a in (
        island_params, outer_params, momentum, path_modules.T, owner_modules.T)]
    home = pl.pallas_call(
        functools.partial(relay, n),
        out_shape=pltpu.VMEM((4, depth, width), f32),
        in_specs=[hbm] * 5,
        out_specs=pl.BlockSpec(memory_space=pltpu.VMEM),
        scratch_shapes=[
            pltpu.SMEM((2, n), jnp.int32),
            pltpu.SMEM((1, n), jnp.int32),
            pltpu.VMEM((depth, width), f32),
            pltpu.VMEM((depth, width), f32),
            pltpu.VMEM((depth, width), f32),
            pltpu.VMEM((chunks, n, depth, cols), f32),
            pltpu.VMEM((chunks, n, 3, depth, cols), f32),
            pltpu.VMEM((n * n, 128), f32),
            pltpu.SMEM((n,), jnp.int32),
            dma((4,)),
        ] + [dma((chunks,))] * 7 + [pltpu.VMEM((n, 3, depth, cols), f32)] * chunks,
        compiler_params=pltpu.CompilerParams(collective_id=1, has_side_effects=True, vmem_limit_bytes=ROOM),
        name="outer_step",
    )(*ins)
    return pl.pallas_call(
        finish,
        out_shape=tuple(jax.ShapeDtypeStruct(a.shape, f32) for a in (island_params, outer_params, momentum)),
        in_specs=[pl.BlockSpec(memory_space=pltpu.VMEM)],
        out_specs=(hbm,) * 3,
        scratch_shapes=[dma((3,))],
        compiler_params=pltpu.CompilerParams(vmem_limit_bytes=ROOM),
        name="finish",
    )(home)


def solution(mesh):
    split = P("island", None, "shard", None)
    return jax.shard_map(
        body,
        mesh=mesh,
        in_specs=(split, split, split, P(), P()),
        out_specs=(split, split, split),
        check_vma=False,
    )
```

```python
import functools

import jax
import jax.numpy as jnp
from jax import lax
from jax.experimental import pallas as pl
from jax.experimental.pallas import tpu as pltpu
from jax.sharding import PartitionSpec as P

momentum_rate = 0.9
outer_rate = 0.7
both_rates = outer_rate * (1.0 + momentum_rate)
MESH = pl.DeviceIdType.MESH
ROOM = 16 * 1024 * 1024
chunks = 2


def relay(n, p_hbm, outer_hbm, mom_hbm, path_hbm, owner_hbm, home,
          path, owner, outer_v, mom_v, mine_v, table, stage, weights, slot_of,
          load_sem, self_sem, send_p, recv_p, send_u, recv_u, *slots):
    arrived = slots[:chunks]
    me = lax.axis_index("island")
    ring = n // 2
    width = outer_v.shape[1]
    cols = width // n // chunks
    far_first = sorted(range(ring), key=lambda d: -min(d, ring - d))
    offsets = [(dz, dx) for dz in far_first for dx in (1, 0) if (dz, dx) != (0, 0)]
    peers = len(offsets)
    z, x = me // 2, me % 2

    def ahead(k):
        dz, dx = offsets[k]
        return lax.rem(z + dz, ring) * 2 + lax.rem(x + dx, 2)

    def behind(k):
        dz, dx = offsets[k]
        return lax.rem(z + ring - dz, ring) * 2 + lax.rem(x + dx, 2)

    def span(j, c):
        return pl.ds(pl.multiple_of(j * (cols * chunks) + c * cols, cols), cols)

    def remote(src, dst, ssem, rsem, k):
        return pltpu.make_async_remote_copy(
            src_ref=src, dst_ref=dst, send_sem=ssem, recv_sem=rsem,
            device_id={"island": ahead(k)}, device_id_type=MESH)

    def deliver(c, t):
        pltpu.make_async_remote_copy(
            src_ref=stage.at[c, t], dst_ref=home.at[0:3, :, span(me, c)], send_sem=send_u.at[c], recv_sem=recv_u.at[c],
            device_id={"island": t}, device_id_type=MESH).start()

    def drain(ref, sem):
        pltpu.make_async_copy(ref, ref, sem).wait()

    small = [pltpu.make_async_copy(path_hbm, path, load_sem.at[0]),
             pltpu.make_async_copy(owner_hbm, owner, load_sem.at[1]),
             pltpu.make_async_copy(outer_hbm.at[0, 0], outer_v, load_sem.at[2]),
             pltpu.make_async_copy(mom_hbm.at[0, 0], mom_v, load_sem.at[3]),
             pltpu.make_async_copy(p_hbm.at[0], mine_v.at[0:2], load_sem.at[4])]
    for copy in small:
        copy.start()
    barrier = pltpu.get_barrier_semaphore()
    for k in range(peers):
        pl.semaphore_signal(barrier, inc=1, device_id={"island": ahead(k)}, device_id_type=MESH)
    for copy in small:
        copy.wait()
    mine = owner[0, me]
    used = jnp.int32(0)
    for j in range(n):
        for level in range(2):
            used += (path[level, j] == mine).astype(jnp.int32)
    hit = jnp.minimum(used, 1).astype(jnp.float32)
    mine_v[2] = (1.0 - both_rates * hit) * outer_v[...] - (
        outer_rate * momentum_rate * momentum_rate) * mom_v[...]
    pl.semaphore_wait(barrier, peers)
    for c in range(chunks):
        for k in range(peers):
            remote(mine_v.at[:, :, span(ahead(k), c)], arrived[c].at[k], send_p.at[c], recv_p.at[c], k).start()
        arrived[c][peers] = mine_v[:, :, span(me, c)]

    sources = [behind(k) for k in range(peers)] + [me]
    for m in range(n):
        level = m // ring
        count = jnp.int32(0)
        holder = jnp.int32(0)
        for k in range(n):
            count += (path[level, sources[k]] == m).astype(jnp.int32)
            holder = jnp.where(owner[0, sources[k]] == m, jnp.int32(k), holder)
        slot_of[m] = holder
        rate = both_rates / jnp.maximum(jnp.full((1, 128), count.astype(jnp.float32)), 1.0)
        for k in range(n):
            weights[pl.ds(m * n + k, 1), :] = rate * (path[level, sources[k]] == m).astype(jnp.float32)

    for c in range(chunks):
        drain(arrived[c].at[0:peers], recv_p.at[c])
        for level in range(2):
            acc = [arrived[c][slot_of[level * ring + m], 2] for m in range(ring)]
            for k in range(n):
                v = arrived[c][k, level]
                for m in range(ring):
                    w = weights[pl.ds((level * ring + m) * n + k, 1), :]
                    if cols > 128:
                        w = jnp.concatenate([w] * (cols // 128), axis=1)
                    acc[m] = acc[m] + w * v
            for m in range(ring):
                table[c, level * ring + m] = acc[m]
        for t in [0, 1, 2, 3, 4, 5, 6, 7, 8, 9, 10, 11, 12, 13, 14, 15]:
            stage[c, t, 0] = table[c, path[0, t]]
            stage[c, t, 1] = table[c, path[1, t]]
            stage[c, t, 2] = table[c, owner[0, t]]

            @pl.when(t != me)
            def _():
                deliver(c, t)
        home[0:3, :, span(me, c)] = stage[c, me]

    for c in range(chunks):
        drain(stage.at[c, 0:peers], recv_u.at[c])
    home[3] = ((outer_v[...] - home[2]) * (1.0 / outer_rate) + momentum_rate * mom_v[...]) * (
        1.0 / (1.0 + momentum_rate))
    for c in range(chunks):
        drain(arrived[c].at[0:peers], send_p.at[c])
        drain(stage.at[c, 0:peers], send_u.at[c])


def finish(home, par_out, outer_out, mom_out, sem):
    stores = [pltpu.make_async_copy(home.at[0:2], par_out.at[0], sem.at[0]),
              pltpu.make_async_copy(home.at[2], outer_out.at[0, 0], sem.at[1]),
              pltpu.make_async_copy(home.at[3], mom_out.at[0, 0], sem.at[2])]
    for copy in stores:
        copy.start()
    for copy in stores:
        copy.wait()


def body(island_params, outer_params, momentum, path_modules, owner_modules):
    n = path_modules.shape[0]
    depth, width = island_params.shape[2:]
    cols = width // n // chunks
    f32 = jnp.float32
    hbm = pl.BlockSpec(memory_space=pltpu.HBM)
    dma = pltpu.SemaphoreType.DMA
    ins = [pltpu.with_memory_space_constraint(a, pltpu.HBM) for a in (
        island_params, outer_params, momentum, path_modules.T, owner_modules.T)]
    home = pl.pallas_call(
        functools.partial(relay, n),
        out_shape=pltpu.VMEM((4, depth, width), f32),
        in_specs=[hbm] * 5,
        out_specs=pl.BlockSpec(memory_space=pltpu.VMEM),
        scratch_shapes=[
            pltpu.SMEM((2, n), jnp.int32),
            pltpu.SMEM((1, n), jnp.int32),
            pltpu.VMEM((depth, width), f32),
            pltpu.VMEM((depth, width), f32),
            pltpu.VMEM((3, depth, width), f32),
            pltpu.VMEM((chunks, n, depth, cols), f32),
            pltpu.VMEM((chunks, n, 3, depth, cols), f32),
            pltpu.VMEM((n * n, 128), f32),
            pltpu.SMEM((n,), jnp.int32),
            dma((5,)),
        ] + [dma((chunks,))] * 5 + [pltpu.VMEM((n, 3, depth, cols), f32)] * chunks,
        compiler_params=pltpu.CompilerParams(collective_id=1, has_side_effects=True, vmem_limit_bytes=ROOM),
        name="outer_step",
    )(*ins)
    return pl.pallas_call(
        finish,
        out_shape=tuple(jax.ShapeDtypeStruct(a.shape, f32) for a in (island_params, outer_params, momentum)),
        in_specs=[pl.BlockSpec(memory_space=pltpu.VMEM)],
        out_specs=(hbm,) * 3,
        scratch_shapes=[dma((3,))],
        compiler_params=pltpu.CompilerParams(vmem_limit_bytes=ROOM),
        name="finish",
    )(home)


def solution(mesh):
    split = P("island", None, "shard", None)
    return jax.shard_map(
        body,
        mesh=mesh,
        in_specs=(split, split, split, P(), P()),
        out_specs=(split, split, split),
        check_vma=False,
    )
```

```python
import functools

import jax
import jax.numpy as jnp
from jax import lax
from jax.experimental import pallas as pl
from jax.experimental.pallas import tpu as pltpu
from jax.sharding import PartitionSpec as P

momentum_rate = 0.9
outer_rate = 0.7
both_rates = outer_rate * (1.0 + momentum_rate)
MESH = pl.DeviceIdType.MESH
ROOM = 16 * 1024 * 1024
chunks = 2


def relay(n, p_hbm, outer_hbm, mom_hbm, path_hbm, owner_hbm, home,
          path, owner, outer_v, mom_v, mine_v, table, stage, weights, slot_of,
          load_sem, self_sem, send_p, recv_p, send_u, recv_u, *slots):
    arrived = slots[:chunks]
    me = lax.axis_index("island")
    core = lax.axis_index("shard") % 2
    ring = n // 2
    width = outer_v.shape[1]
    cols = width // n // chunks
    far_first = sorted(range(ring), key=lambda d: -min(d, ring - d))
    offsets = [(dz, dx) for dz in far_first for dx in (1, 0) if (dz, dx) != (0, 0)]
    peers = len(offsets)
    z, x = me // 2, me % 2

    def ahead(k):
        dz, dx = offsets[k]
        return lax.rem(z + dz, ring) * 2 + lax.rem(x + dx, 2)

    def behind(k):
        dz, dx = offsets[k]
        return lax.rem(z + ring - dz, ring) * 2 + lax.rem(x + dx, 2)

    def span(j, c):
        return pl.ds(pl.multiple_of(j * (cols * chunks) + c * cols, cols), cols)

    def remote(src, dst, ssem, rsem, k):
        return pltpu.make_async_remote_copy(
            src_ref=src, dst_ref=dst, send_sem=ssem, recv_sem=rsem,
            device_id={"island": ahead(k)}, device_id_type=MESH)

    def deliver(c, t):
        pltpu.make_async_remote_copy(
            src_ref=stage.at[c, t], dst_ref=home.at[0:3, :, span(me, c)], send_sem=send_u.at[c], recv_sem=recv_u.at[c],
            device_id={"island": t}, device_id_type=MESH).start()

    def drain(ref, sem):
        pltpu.make_async_copy(ref, ref, sem).wait()

    small = [pltpu.make_async_copy(path_hbm, path, load_sem.at[0]),
             pltpu.make_async_copy(owner_hbm, owner, load_sem.at[1]),
             pltpu.make_async_copy(outer_hbm.at[0, 0], outer_v, load_sem.at[2]),
             pltpu.make_async_copy(mom_hbm.at[0, 0], mom_v, load_sem.at[3]),
             pltpu.make_async_copy(p_hbm.at[0], mine_v.at[0:2], load_sem.at[4])]
    for copy in small:
        copy.start()
    barrier = pltpu.get_barrier_semaphore()
    for k in range(peers):
        pl.semaphore_signal(barrier, inc=1, device_id={"island": ahead(k)}, device_id_type=MESH)
    for copy in small:
        copy.wait()
    mine = owner[0, me]
    used = jnp.int32(0)
    for j in range(n):
        for level in range(2):
            used += (path[level, j] == mine).astype(jnp.int32)
    hit = jnp.minimum(used, 1).astype(jnp.float32)
    mine_v[2] = (1.0 - both_rates * hit) * outer_v[...] - (
        outer_rate * momentum_rate * momentum_rate) * mom_v[...]
    pl.semaphore_wait(barrier, peers)
    for c in range(chunks):
        if c == 1:
            @pl.when(core == 1)
            def _():
                drain(arrived[0].at[0:peers], send_p.at[0])

        for k in range(peers):
            remote(mine_v.at[:, :, span(ahead(k), c)], arrived[c].at[k], send_p.at[c], recv_p.at[c], k).start()
        arrived[c][peers] = mine_v[:, :, span(me, c)]

    sources = [behind(k) for k in range(peers)] + [me]
    for m in range(n):
        level = m // ring
        count = jnp.int32(0)
        holder = jnp.int32(0)
        for k in range(n):
            count += (path[level, sources[k]] == m).astype(jnp.int32)
            holder = jnp.where(owner[0, sources[k]] == m, jnp.int32(k), holder)
        slot_of[m] = holder
        rate = both_rates / jnp.maximum(jnp.full((1, 128), count.astype(jnp.float32)), 1.0)
        for k in range(n):
            weights[pl.ds(m * n + k, 1), :] = rate * (path[level, sources[k]] == m).astype(jnp.float32)

    for c in range(chunks):
        drain(arrived[c].at[0:peers], recv_p.at[c])
        for level in range(2):
            acc = [arrived[c][slot_of[level * ring + m], 2] for m in range(ring)]
            for k in range(n):
                v = arrived[c][k, level]
                for m in range(ring):
                    w = weights[pl.ds((level * ring + m) * n + k, 1), :]
                    if cols > 128:
                        w = jnp.concatenate([w] * (cols // 128), axis=1)
                    acc[m] = acc[m] + w * v
            for m in range(ring):
                table[c, level * ring + m] = acc[m]
        for t in [0, 1, 2, 3, 4, 5, 6, 7, 8, 9, 10, 11, 12, 13, 14, 15]:
            stage[c, t, 0] = table[c, path[0, t]]
            stage[c, t, 1] = table[c, path[1, t]]
            stage[c, t, 2] = table[c, owner[0, t]]

            @pl.when(t != me)
            def _():
                deliver(c, t)
        home[0:3, :, span(me, c)] = stage[c, me]

    for c in range(chunks):
        drain(stage.at[c, 0:peers], recv_u.at[c])
    home[3] = ((outer_v[...] - home[2]) * (1.0 / outer_rate) + momentum_rate * mom_v[...]) * (
        1.0 / (1.0 + momentum_rate))
    for c in range(chunks):
        if c == 0:
            @pl.when(core == 0)
            def _():
                drain(arrived[c].at[0:peers], send_p.at[c])
        else:
            drain(arrived[c].at[0:peers], send_p.at[c])
        drain(stage.at[c, 0:peers], send_u.at[c])


def finish(home, par_out, outer_out, mom_out, sem):
    stores = [pltpu.make_async_copy(home.at[0:2], par_out.at[0], sem.at[0]),
              pltpu.make_async_copy(home.at[2], outer_out.at[0, 0], sem.at[1]),
              pltpu.make_async_copy(home.at[3], mom_out.at[0, 0], sem.at[2])]
    for copy in stores:
        copy.start()
    for copy in stores:
        copy.wait()


def body(island_params, outer_params, momentum, path_modules, owner_modules):
    n = path_modules.shape[0]
    depth, width = island_params.shape[2:]
    cols = width // n // chunks
    f32 = jnp.float32
    hbm = pl.BlockSpec(memory_space=pltpu.HBM)
    dma = pltpu.SemaphoreType.DMA
    ins = [pltpu.with_memory_space_constraint(a, pltpu.HBM) for a in (
        island_params, outer_params, momentum, path_modules.T, owner_modules.T)]
    home = pl.pallas_call(
        functools.partial(relay, n),
        out_shape=pltpu.VMEM((4, depth, width), f32),
        in_specs=[hbm] * 5,
        out_specs=pl.BlockSpec(memory_space=pltpu.VMEM),
        scratch_shapes=[
            pltpu.SMEM((2, n), jnp.int32),
            pltpu.SMEM((1, n), jnp.int32),
            pltpu.VMEM((depth, width), f32),
            pltpu.VMEM((depth, width), f32),
            pltpu.VMEM((3, depth, width), f32),
            pltpu.VMEM((chunks, n, depth, cols), f32),
            pltpu.VMEM((chunks, n, 3, depth, cols), f32),
            pltpu.VMEM((n * n, 128), f32),
            pltpu.SMEM((n,), jnp.int32),
            dma((5,)),
        ] + [dma((chunks,))] * 5 + [pltpu.VMEM((n, 3, depth, cols), f32)] * chunks,
        compiler_params=pltpu.CompilerParams(collective_id=1, has_side_effects=True, vmem_limit_bytes=ROOM),
        name="outer_step",
    )(*ins)
    return pl.pallas_call(
        finish,
        out_shape=tuple(jax.ShapeDtypeStruct(a.shape, f32) for a in (island_params, outer_params, momentum)),
        in_specs=[pl.BlockSpec(memory_space=pltpu.VMEM)],
        out_specs=(hbm,) * 3,
        scratch_shapes=[dma((3,))],
        compiler_params=pltpu.CompilerParams(vmem_limit_bytes=ROOM),
        name="finish",
    )(home)


def solution(mesh):
    split = P("island", None, "shard", None)
    return jax.shard_map(
        body,
        mesh=mesh,
        in_specs=(split, split, split, P(), P()),
        out_specs=(split, split, split),
        check_vma=False,
    )
```

```python
import functools

import jax
import jax.numpy as jnp
from jax import lax
from jax.experimental import pallas as pl
from jax.experimental.pallas import tpu as pltpu
from jax.sharding import PartitionSpec as P

momentum_rate = 0.9
outer_rate = 0.7
both_rates = outer_rate * (1.0 + momentum_rate)
MESH = pl.DeviceIdType.MESH
ROOM = 16 * 1024 * 1024
chunks = 2


def relay(n, p_hbm, outer_hbm, mom_hbm, path_hbm, owner_hbm, home,
          path, owner, outer_v, mom_v, mine_v, table, stage, weights, slot_of,
          load_sem, self_sem, send_p, recv_p, send_u, recv_u, *slots):
    arrived = slots[:chunks]
    me = lax.axis_index("island")
    core = lax.axis_index("shard") % 2
    ring = n // 2
    width = outer_v.shape[1]
    cols = width // n // chunks
    far_first = sorted(range(ring), key=lambda d: -min(d, ring - d))
    offsets = [(dz, dx) for dz in far_first for dx in (1, 0) if (dz, dx) != (0, 0)]
    peers = len(offsets)
    z, x = me // 2, me % 2

    def ahead(k):
        dz, dx = offsets[k]
        turn = jnp.where(core == 1, ring - dz, dz)
        return lax.rem(z + turn, ring) * 2 + lax.rem(x + dx, 2)

    def behind(k):
        dz, dx = offsets[k]
        turn = jnp.where(core == 1, dz, ring - dz)
        return lax.rem(z + turn, ring) * 2 + lax.rem(x + dx, 2)

    def span(j, c):
        return pl.ds(pl.multiple_of(j * (cols * chunks) + c * cols, cols), cols)

    def remote(src, dst, ssem, rsem, k):
        return pltpu.make_async_remote_copy(
            src_ref=src, dst_ref=dst, send_sem=ssem, recv_sem=rsem,
            device_id={"island": ahead(k)}, device_id_type=MESH)

    def deliver(c, t):
        pltpu.make_async_remote_copy(
            src_ref=stage.at[c, t], dst_ref=home.at[0:3, :, span(me, c)], send_sem=send_u.at[c], recv_sem=recv_u.at[c],
            device_id={"island": t}, device_id_type=MESH).start()

    def drain(ref, sem):
        pltpu.make_async_copy(ref, ref, sem).wait()

    small = [pltpu.make_async_copy(path_hbm, path, load_sem.at[0]),
             pltpu.make_async_copy(owner_hbm, owner, load_sem.at[1]),
             pltpu.make_async_copy(outer_hbm.at[0, 0], outer_v, load_sem.at[2]),
             pltpu.make_async_copy(mom_hbm.at[0, 0], mom_v, load_sem.at[3]),
             pltpu.make_async_copy(p_hbm.at[0], mine_v.at[0:2], load_sem.at[4])]
    for copy in small:
        copy.start()
    barrier = pltpu.get_barrier_semaphore()
    for k in range(peers):
        pl.semaphore_signal(barrier, inc=1, device_id={"island": ahead(k)}, device_id_type=MESH)
    for copy in small:
        copy.wait()
    mine = owner[0, me]
    used = jnp.int32(0)
    for j in range(n):
        for level in range(2):
            used += (path[level, j] == mine).astype(jnp.int32)
    hit = jnp.minimum(used, 1).astype(jnp.float32)
    mine_v[2] = (1.0 - both_rates * hit) * outer_v[...] - (
        outer_rate * momentum_rate * momentum_rate) * mom_v[...]
    pl.semaphore_wait(barrier, peers)
    for c in range(chunks):
        if c == 1:
            @pl.when(core == 1)
            def _():
                drain(arrived[0].at[0:peers], send_p.at[0])

        for k in range(peers):
            remote(mine_v.at[:, :, span(ahead(k), c)], arrived[c].at[k], send_p.at[c], recv_p.at[c], k).start()
        arrived[c][peers] = mine_v[:, :, span(me, c)]

    sources = [behind(k) for k in range(peers)] + [me]
    for m in range(n):
        level = m // ring
        count = jnp.int32(0)
        holder = jnp.int32(0)
        for k in range(n):
            count += (path[level, sources[k]] == m).astype(jnp.int32)
            holder = jnp.where(owner[0, sources[k]] == m, jnp.int32(k), holder)
        slot_of[m] = holder
        rate = both_rates / jnp.maximum(jnp.full((1, 128), count.astype(jnp.float32)), 1.0)
        for k in range(n):
            weights[pl.ds(m * n + k, 1), :] = rate * (path[level, sources[k]] == m).astype(jnp.float32)

    for c in range(chunks):
        drain(arrived[c].at[0:peers], recv_p.at[c])
        for level in range(2):
            acc = [arrived[c][slot_of[level * ring + m], 2] for m in range(ring)]
            for k in range(n):
                v = arrived[c][k, level]
                for m in range(ring):
                    w = weights[pl.ds((level * ring + m) * n + k, 1), :]
                    if cols > 128:
                        w = jnp.concatenate([w] * (cols // 128), axis=1)
                    acc[m] = acc[m] + w * v
            for m in range(ring):
                table[c, level * ring + m] = acc[m]
        for t in [0, 1, 2, 3, 4, 5, 6, 7, 8, 9, 10, 11, 12, 13, 14, 15]:
            stage[c, t, 0] = table[c, path[0, t]]
            stage[c, t, 1] = table[c, path[1, t]]
            stage[c, t, 2] = table[c, owner[0, t]]

            @pl.when(t != me)
            def _():
                deliver(c, t)
        home[0:3, :, span(me, c)] = stage[c, me]

    for c in range(chunks):
        drain(stage.at[c, 0:peers], recv_u.at[c])
        for j in range(n):
            there = span(j, c)
            home[3, :, there] = ((outer_v[:, there] - home[2, :, there]) * (1.0 / outer_rate)
                                 + momentum_rate * mom_v[:, there]) * (1.0 / (1.0 + momentum_rate))
    for c in range(chunks):
        if c == 0:
            @pl.when(core == 0)
            def _():
                drain(arrived[c].at[0:peers], send_p.at[c])
        else:
            drain(arrived[c].at[0:peers], send_p.at[c])
        drain(stage.at[c, 0:peers], send_u.at[c])


def finish(home, par_out, outer_out, mom_out, sem):
    stores = [pltpu.make_async_copy(home.at[0:2], par_out.at[0], sem.at[0]),
              pltpu.make_async_copy(home.at[2], outer_out.at[0, 0], sem.at[1]),
              pltpu.make_async_copy(home.at[3], mom_out.at[0, 0], sem.at[2])]
    for copy in stores:
        copy.start()
    for copy in stores:
        copy.wait()


def body(island_params, outer_params, momentum, path_modules, owner_modules):
    n = path_modules.shape[0]
    depth, width = island_params.shape[2:]
    cols = width // n // chunks
    f32 = jnp.float32
    hbm = pl.BlockSpec(memory_space=pltpu.HBM)
    dma = pltpu.SemaphoreType.DMA
    ins = [pltpu.with_memory_space_constraint(a, pltpu.HBM) for a in (
        island_params, outer_params, momentum, path_modules.T, owner_modules.T)]
    home = pl.pallas_call(
        functools.partial(relay, n),
        out_shape=pltpu.VMEM((4, depth, width), f32),
        in_specs=[hbm] * 5,
        out_specs=pl.BlockSpec(memory_space=pltpu.VMEM),
        scratch_shapes=[
            pltpu.SMEM((2, n), jnp.int32),
            pltpu.SMEM((1, n), jnp.int32),
            pltpu.VMEM((depth, width), f32),
            pltpu.VMEM((depth, width), f32),
            pltpu.VMEM((3, depth, width), f32),
            pltpu.VMEM((chunks, n, depth, cols), f32),
            pltpu.VMEM((chunks, n, 3, depth, cols), f32),
            pltpu.VMEM((n * n, 128), f32),
            pltpu.SMEM((n,), jnp.int32),
            dma((5,)),
        ] + [dma((chunks,))] * 5 + [pltpu.VMEM((n, 3, depth, cols), f32)] * chunks,
        compiler_params=pltpu.CompilerParams(collective_id=1, has_side_effects=True, vmem_limit_bytes=ROOM),
        name="outer_step",
    )(*ins)
    return pl.pallas_call(
        finish,
        out_shape=tuple(jax.ShapeDtypeStruct(a.shape, f32) for a in (island_params, outer_params, momentum)),
        in_specs=[pl.BlockSpec(memory_space=pltpu.VMEM)],
        out_specs=(hbm,) * 3,
        scratch_shapes=[dma((3,))],
        compiler_params=pltpu.CompilerParams(vmem_limit_bytes=ROOM),
        name="finish",
    )(home)


def solution(mesh):
    split = P("island", None, "shard", None)
    return jax.shard_map(
        body,
        mesh=mesh,
        in_specs=(split, split, split, P(), P()),
        out_specs=(split, split, split),
        check_vma=False,
    )
```

```python
import functools

import jax
import jax.numpy as jnp
from jax import lax
from jax.experimental import pallas as pl
from jax.experimental.pallas import tpu as pltpu
from jax.sharding import PartitionSpec as P

momentum_rate = 0.9
outer_rate = 0.7
both_rates = outer_rate * (1.0 + momentum_rate)
MESH = pl.DeviceIdType.MESH
ROOM = 16 * 1024 * 1024
chunks = 2


def relay(n, p_hbm, outer_hbm, mom_hbm, path_hbm, owner_hbm, home,
          path, owner, outer_v, mom_v, mine_v, table, stage, weights, slot_of,
          load_sem, self_sem, send_p, recv_p, send_u, recv_u, *slots):
    arrived = slots[:chunks]
    me = lax.axis_index("island")
    core = lax.axis_index("shard") % 2
    ring = n // 2
    width = outer_v.shape[1]
    cols = width // n // chunks
    far_first = sorted(range(ring), key=lambda d: -min(d, ring - d))
    offsets = [(dz, dx) for dz in far_first for dx in (1, 0) if (dz, dx) != (0, 0)]
    peers = len(offsets)
    z, x = me // 2, me % 2

    def ahead(k):
        dz, dx = offsets[k]
        turn = jnp.where(core == 1, ring - dz, dz)
        return lax.rem(z + turn, ring) * 2 + lax.rem(x + dx, 2)

    def behind(k):
        dz, dx = offsets[k]
        turn = jnp.where(core == 1, dz, ring - dz)
        return lax.rem(z + turn, ring) * 2 + lax.rem(x + dx, 2)

    def span(j, c):
        return pl.ds(pl.multiple_of(j * (cols * chunks) + c * cols, cols), cols)

    def remote(src, dst, ssem, rsem, k):
        return pltpu.make_async_remote_copy(
            src_ref=src, dst_ref=dst, send_sem=ssem, recv_sem=rsem,
            device_id={"island": ahead(k)}, device_id_type=MESH)

    def deliver(c, i, to):
        pltpu.make_async_remote_copy(
            src_ref=stage.at[c, i], dst_ref=home.at[0:3, :, span(me, c)], send_sem=send_u.at[c], recv_sem=recv_u.at[c],
            device_id={"island": to}, device_id_type=MESH).start()

    def drain(ref, sem):
        pltpu.make_async_copy(ref, ref, sem).wait()

    small = [pltpu.make_async_copy(path_hbm, path, load_sem.at[0]),
             pltpu.make_async_copy(owner_hbm, owner, load_sem.at[1]),
             pltpu.make_async_copy(outer_hbm.at[0, 0], outer_v, load_sem.at[2]),
             pltpu.make_async_copy(mom_hbm.at[0, 0], mom_v, load_sem.at[3]),
             pltpu.make_async_copy(p_hbm.at[0], mine_v.at[0:2], load_sem.at[4])]
    for copy in small:
        copy.start()
    barrier = pltpu.get_barrier_semaphore()
    for k in range(peers):
        pl.semaphore_signal(barrier, inc=1, device_id={"island": ahead(k)}, device_id_type=MESH)
    for copy in small:
        copy.wait()
    mine = owner[0, me]
    used = jnp.int32(0)
    for j in range(n):
        for level in range(2):
            used += (path[level, j] == mine).astype(jnp.int32)
    hit = jnp.minimum(used, 1).astype(jnp.float32)
    mine_v[2] = (1.0 - both_rates * hit) * outer_v[...] - (
        outer_rate * momentum_rate * momentum_rate) * mom_v[...]
    pl.semaphore_wait(barrier, peers)
    for c in range(chunks):
        if c == 1:
            @pl.when(core == 1)
            def _():
                drain(arrived[0].at[0:peers], send_p.at[0])

        for k in range(peers):
            remote(mine_v.at[:, :, span(ahead(k), c)], arrived[c].at[k], send_p.at[c], recv_p.at[c], k).start()
        arrived[c][peers] = mine_v[:, :, span(me, c)]

    sources = [behind(k) for k in range(peers)] + [me]
    for m in range(n):
        level = m // ring
        count = jnp.int32(0)
        holder = jnp.int32(0)
        for k in range(n):
            count += (path[level, sources[k]] == m).astype(jnp.int32)
            holder = jnp.where(owner[0, sources[k]] == m, jnp.int32(k), holder)
        slot_of[m] = holder
        rate = both_rates / jnp.maximum(jnp.full((1, 128), count.astype(jnp.float32)), 1.0)
        for k in range(n):
            weights[pl.ds(m * n + k, 1), :] = rate * (path[level, sources[k]] == m).astype(jnp.float32)

    for c in range(chunks):
        drain(arrived[c].at[0:peers], recv_p.at[c])
        for level in range(2):
            acc = [arrived[c][slot_of[level * ring + m], 2] for m in range(ring)]
            for k in range(n):
                v = arrived[c][k, level]
                for m in range(ring):
                    w = weights[pl.ds((level * ring + m) * n + k, 1), :]
                    if cols > 128:
                        w = jnp.concatenate([w] * (cols // 128), axis=1)
                    acc[m] = acc[m] + w * v
            for m in range(ring):
                table[c, level * ring + m] = acc[m]
        orders = (([0, 1, 2, 3, 4, 5, 6, 7, 8, 9, 10, 11, 12, 13, 14, 15], [0, 1, 2, 3, 4, 5, 6, 7, 8, 9, 10, 11, 12, 13, 14, 15]),
                  ([0, 1, 2, 3, 8, 9, 10, 11, 12, 13, 14, 15, 4, 5, 6, 7], [0, 1, 2, 3, 4, 5, 6, 7, 8, 9, 10, 11, 12, 13, 14, 15]))
        for i, (early, late) in enumerate(zip(*orders[c])):
            to = jnp.where(me < n // 2, early, late)
            stage[c, i, 0] = table[c, path[0, to]]
            stage[c, i, 1] = table[c, path[1, to]]
            stage[c, i, 2] = table[c, owner[0, to]]

            @pl.when(to != me)
            def _():
                deliver(c, i, to)

        home[0, :, span(me, c)] = table[c, path[0, me]]
        home[1, :, span(me, c)] = table[c, path[1, me]]
        home[2, :, span(me, c)] = table[c, owner[0, me]]

    for c in range(chunks):
        drain(stage.at[c, 0:peers], recv_u.at[c])
    home[3] = ((outer_v[...] - home[2]) * (1.0 / outer_rate) + momentum_rate * mom_v[...]) * (
        1.0 / (1.0 + momentum_rate))
    for c in range(chunks):
        if c == 0:
            @pl.when(core == 0)
            def _():
                drain(arrived[c].at[0:peers], send_p.at[c])
        else:
            drain(arrived[c].at[0:peers], send_p.at[c])
        drain(stage.at[c, 0:peers], send_u.at[c])


def finish(home, par_out, outer_out, mom_out, sem):
    stores = [pltpu.make_async_copy(home.at[0:2], par_out.at[0], sem.at[0]),
              pltpu.make_async_copy(home.at[2], outer_out.at[0, 0], sem.at[1]),
              pltpu.make_async_copy(home.at[3], mom_out.at[0, 0], sem.at[2])]
    for copy in stores:
        copy.start()
    for copy in stores:
        copy.wait()


def body(island_params, outer_params, momentum, path_modules, owner_modules):
    n = path_modules.shape[0]
    depth, width = island_params.shape[2:]
    cols = width // n // chunks
    f32 = jnp.float32
    hbm = pl.BlockSpec(memory_space=pltpu.HBM)
    dma = pltpu.SemaphoreType.DMA
    ins = [pltpu.with_memory_space_constraint(a, pltpu.HBM) for a in (
        island_params, outer_params, momentum, path_modules.T, owner_modules.T)]
    home = pl.pallas_call(
        functools.partial(relay, n),
        out_shape=pltpu.VMEM((4, depth, width), f32),
        in_specs=[hbm] * 5,
        out_specs=pl.BlockSpec(memory_space=pltpu.VMEM),
        scratch_shapes=[
            pltpu.SMEM((2, n), jnp.int32),
            pltpu.SMEM((1, n), jnp.int32),
            pltpu.VMEM((depth, width), f32),
            pltpu.VMEM((depth, width), f32),
            pltpu.VMEM((3, depth, width), f32),
            pltpu.VMEM((chunks, n, depth, cols), f32),
            pltpu.VMEM((chunks, n, 3, depth, cols), f32),
            pltpu.VMEM((n * n, 128), f32),
            pltpu.SMEM((n,), jnp.int32),
            dma((5,)),
        ] + [dma((chunks,))] * 5 + [pltpu.VMEM((n, 3, depth, cols), f32)] * chunks,
        compiler_params=pltpu.CompilerParams(collective_id=1, has_side_effects=True, vmem_limit_bytes=ROOM),
        name="outer_step",
    )(*ins)
    return pl.pallas_call(
        finish,
        out_shape=tuple(jax.ShapeDtypeStruct(a.shape, f32) for a in (island_params, outer_params, momentum)),
        in_specs=[pl.BlockSpec(memory_space=pltpu.VMEM)],
        out_specs=(hbm,) * 3,
        scratch_shapes=[dma((3,))],
        compiler_params=pltpu.CompilerParams(vmem_limit_bytes=ROOM),
        name="finish",
    )(home)


def solution(mesh):
    split = P("island", None, "shard", None)
    return jax.shard_map(
        body,
        mesh=mesh,
        in_specs=(split, split, split, P(), P()),
        out_specs=(split, split, split),
        check_vma=False,
    )
```
